32 devices in a mesh: pix: 8 (over y, x, core), chan: 4 (over z).
Axes of the slice: x: 2, y: 2, z: 4, core: 2. Of those that a mesh axis runs over, the one named last changes fastest.
Arguments:
- counts: int32 [131072, 1024], P('pix', 'chan'), may hold values from 0 to 11
- templates: float32 [16, 131072], P(None, 'pix'), may hold values from 0.05 to 1
- spectra: float32 [16, 1024], replicated, may hold values from 0.0045 to 1
- response: float32 [1024, 1024], P(None, 'chan'), may hold values from 0.0001953125 to 0.3
- psf_shape: float32 [32, 65], replicated, may hold values from 0.05 to 1
- widths: int32 [32], replicated, may hold values from 1 to 32, as said below
Outputs:
- new_templates: float32 [16, 131072], P(None, 'pix')
- new_spectra: float32 [16, 1024], replicated
The draws below stay inside these ranges and needn't reach their ends.
Inputs may be any that keep to these rules, and one draw needn't show every extreme that they name: `widths`: one band has half width exactly 32.
All inputs are finite; a program needn't handle non-finite values.
Results may differ from the reference program's by a relative error of at most 0.0001.
Values sent between devices are 32-bit elements; how exact they have to be, the bound alone decides.
A program may use at most 128 MiB of HBM per device.

```python
import math
import jax
import jax.numpy as jnp
from jax import lax

K = 16
NCH = 1024
CB = 32
HW = 32
TAPS = 65
NBAND = 32
NPIX = 131072


def draw_widths(key, part):
    draw_key, spot_key = jax.random.split(key)
    chosen = jax.random.randint(draw_key, (NBAND,), 1, HW + 1)
    spot_at = jax.random.randint(spot_key, (), 0, NBAND)
    return jnp.where(jnp.arange(NBAND) == spot_at, HW, chosen).astype(jnp.int32)


def draw_counts(key, part):
    levels = jax.random.randint(key, (NPIX, NCH), 0, 176)
    photons = jnp.where(levels < 11, levels + 1, 0)
    return photons.at[0, 0].set(11).astype(jnp.int32)


def draw_spectra(key, part):
    level_key, block_key = jax.random.split(jax.random.fold_in(key, 31))
    low = jnp.log(jnp.float32(0.03))
    element = jnp.exp(jax.random.uniform(level_key, (K, NCH), jnp.float32, low, 0.0))
    picks = jax.random.randint(block_key, (K, NBAND), 0, 2)
    factor = jnp.where(picks == 1, jnp.float32(1.0), jnp.float32(0.15))
    return (element * jnp.repeat(factor, CB, axis=1)).astype(jnp.float32)


def draw_response(key, part):
    floor_key, peak_key = jax.random.split(jax.random.fold_in(key, 57))
    energy = jnp.arange(NCH, dtype=jnp.int32)[:, None]
    channel = jnp.arange(NCH, dtype=jnp.int32)[None, :]
    near = jnp.abs(energy - channel) <= 2
    floor = jax.random.uniform(floor_key, (NCH, NCH), jnp.float32, 0.2, 1.0) / NCH
    peak = jax.random.uniform(peak_key, (NCH, NCH), jnp.float32, 0.1, 0.3)
    return jnp.where(near, peak, floor).astype(jnp.float32)


def shard_levels(stream_key, dims, cuts, low, high):
    gain = 1.0
    for axis_at, blocks in cuts:
        draws = jax.random.uniform(jax.random.fold_in(jax.random.fold_in(stream_key, 6), axis_at), (blocks,), jnp.float32, low / len(cuts), high / len(cuts))
        gain = gain * jnp.repeat(jnp.exp(draws), dims[axis_at] // blocks).reshape((-1,) + (1,) * (len(dims) - 1 - axis_at))
    return gain


def setup_inputs(seed: int = 0) -> dict:
    splits = jax.random.split(jax.random.key(seed), 7)
    counts = draw_counts(jax.random.fold_in(splits[6], 71), 0)
    templates = jnp.clip(jnp.exp(math.log(1.0) - 2.9957323 * jax.random.uniform(splits[1], (K, NPIX), jnp.float32) ** shard_levels(splits[1], (K, NPIX), ((1, 8),), -0.2, 0.2)), 0.05, 1.0)
    spectra = draw_spectra(jax.random.fold_in(splits[6], 71), 0)
    response = draw_response(jax.random.fold_in(splits[6], 71), 0)
    psf_shape = jnp.clip(jnp.exp(jax.random.uniform(splits[4], (NBAND, TAPS), jnp.float32, math.log(0.05), math.log(1.0))), 0.05, 1.0)
    widths = draw_widths(jax.random.fold_in(splits[6], 71), 0)
    return {"counts": counts, "templates": templates, "spectra": spectra, "response": response, "psf_shape": psf_shape, "widths": widths}


def correlate(signal, kernel):
    return lax.conv_general_dilated(signal, kernel, (1,), "VALID", dimension_numbers=("NCH", "OIH", "NCH"), precision=lax.Precision.HIGHEST)


def kernels(psf_shape, widths):
    offsets = jnp.arange(TAPS, dtype=jnp.int32) - HW
    in_band = jnp.abs(offsets)[None, :] <= widths[:, None]
    unscaled = jnp.where(in_band, psf_shape, jnp.float32(0.0))
    return unscaled / jnp.sum(unscaled, axis=1, keepdims=True)


def reference(counts, templates, spectra, response, psf_shape, widths):
    high = lax.Precision.HIGHEST
    kernel = kernels(psf_shape, widths)
    folded = jnp.dot(spectra, response, precision=high)
    pixel_count = templates.shape[1]
    padded = jnp.pad(templates, ((0, 0), (HW, HW)))
    inside = jnp.pad(jnp.ones((pixel_count,), jnp.float32), (HW, HW))

    def band_step(sums_so_far, band_index):
        num_map, den_map = sums_so_far
        kernel_row = lax.dynamic_index_in_dim(kernel, band_index, 0, keepdims=False)
        folded_band = lax.dynamic_slice_in_dim(folded, band_index * CB, CB, 1)
        observed = lax.dynamic_slice_in_dim(counts, band_index * CB, CB, 1).astype(jnp.float32)
        blurred = correlate(padded[:, None, :], kernel_row[::-1][None, None, :])[:, 0, :]
        predicted = jnp.dot(blurred.T, folded_band, precision=high)
        ratios = observed / predicted
        numerators = jnp.dot(blurred, ratios, precision=high)
        totals_band = jnp.sum(blurred, axis=1)
        back_proj = jnp.dot(folded_band, ratios.T, precision=high)
        back_pad = jnp.pad(back_proj, ((0, 0), (HW, HW)))
        num_map = num_map + correlate(back_pad[:, None, :], kernel_row[None, None, :])[:, 0, :]
        kernel_mass = correlate(inside[None, None, :], kernel_row[None, None, :])[0, 0, :]
        den_map = den_map + jnp.sum(folded_band, axis=1)[:, None] * kernel_mass[None, :]
        return (num_map, den_map), (numerators, totals_band)

    empty_map = jnp.zeros(templates.shape, jnp.float32)
    (num_map, den_map), (numerators, totals_band) = lax.scan(band_step, (empty_map, empty_map), jnp.arange(NBAND, dtype=jnp.int32))
    numer_all = jnp.transpose(numerators, (1, 0, 2)).reshape(K, NCH)
    totals = jnp.repeat(totals_band.T, CB, axis=1)
    num_spec = jnp.dot(numer_all, response.T, precision=high)
    den_spec = jnp.dot(totals, response.T, precision=high)
    new_spectra = spectra * num_spec / den_spec
    new_templates = templates * num_map / den_map
    return new_templates, new_spectra
```

```python
import functools

import jax
import jax.numpy as jnp
from jax import lax
from jax.experimental import pallas as pl
from jax.experimental.pallas import tpu as pltpu
from jax.sharding import PartitionSpec as P

K = 16
CB = 32
HW = 32
TAPS = 65
LB = 128


def kernels(psf_shape, widths):
    offsets = jnp.arange(TAPS, dtype=jnp.int32) - HW
    in_band = jnp.abs(offsets)[None, :] <= widths[:, None]
    unscaled = jnp.where(in_band, psf_shape, jnp.float32(0.0))
    return unscaled / jnp.sum(unscaled, axis=1, keepdims=True)


def split(x):
    hi = x.astype(jnp.bfloat16)
    lo = (x - hi.astype(jnp.float32)).astype(jnp.bfloat16)
    return hi, lo


def dot(a, b, contract):
    return lax.dot_general(a, b, (contract, ((), ())), preferred_element_type=jnp.float32)


def dot3(a, b, contract):
    rows = a[0].shape[0]
    both = dot(jnp.concatenate([a[0], a[1]], axis=0), b[0], contract)
    return both[:rows] + both[rows:] + dot(a[0], b[1], contract)


def sweep_kernel(bands, tile, tp_ref, krev_ref, fold_ref, counts_ref, ext_ref, num_ref, tot_ref,
                 bhi, blo, fhl):
    step = pl.program_id(0)
    blocks = tile // LB
    rows = bands * K

    @pl.when(step == 0)
    def _():
        for b in range(bands):
            grid = jnp.broadcast_to(krev_ref[b : b + 1, :], (LB, 2 * LB))
            skew = pltpu.roll(grid, 0, 1, stride=1, stride_axis=0)
            hi, lo = split(skew)
            bhi[b * LB : (b + 1) * LB, :] = hi
            blo[b * LB : (b + 1) * LB, :] = lo
        fhi, flo = split(fold_ref[...])
        fhl[0:rows, :] = fhi
        fhl[rows : 2 * rows, :] = flo
        ext_ref[...] = jnp.zeros_like(ext_ref)
        num_ref[...] = jnp.zeros_like(num_ref)
        tot_ref[...] = jnp.zeros_like(tot_ref)

    at = pl.multiple_of(step * tile, tile)
    strip = tp_ref[:, pl.ds(at, tile + LB)]
    win = jnp.concatenate([strip[:, n * LB : (n + 2) * LB] for n in range(blocks)], axis=0)
    blur = dot3(split(win), (bhi[...], blo[...]), ((1,), (1,)))
    x = jnp.concatenate(
        [
            jnp.concatenate(
                [blur[n * K : (n + 1) * K, b * LB : (b + 1) * LB] for n in range(blocks)], axis=1
            )
            for b in range(bands)
        ],
        axis=0,
    )
    tot = x[:, 0:LB]
    for n in range(1, blocks):
        tot = tot + x[:, n * LB : (n + 1) * LB]
    tot_ref[...] += tot
    xs = split(x)
    fhi = fhl[0:rows, :]
    flo = fhl[rows : 2 * rows, :]
    xt = jnp.concatenate([xs[0], xs[1]], axis=0)
    predicted = dot(xt, jnp.concatenate([fhi, fhi], axis=0), ((0,), (0,))) + dot(
        xs[0], flo, ((0,), (0,))
    )
    ratios = split(counts_ref[...].astype(jnp.float32) / predicted)
    num_ref[...] += dot3(xs, ratios, ((1,), (0,)))
    back = dot3((fhi, flo), ratios, ((1,), (1,)))
    rearranged = jnp.concatenate(
        [
            jnp.concatenate(
                [back[b * K : (b + 1) * K, n * LB : (n + 1) * LB] for b in range(bands)], axis=1
            )
            for n in range(blocks)
        ],
        axis=0,
    )
    spread = dot3(split(rearranged), (bhi[...], blo[...]), ((1,), (0,)))
    pieces = []
    for n in range(blocks + 1):
        left = spread[n * K : (n + 1) * K, 0:LB] if n < blocks else None
        right = spread[(n - 1) * K : n * K, LB : 2 * LB] if n > 0 else None
        pieces.append(left if right is None else right if left is None else left + right)
    ext_ref[:, pl.ds(at, tile + LB)] += jnp.concatenate(pieces, axis=1)


def sweep(tp, krev, fold, counts, tile):
    pixels, channels = counts.shape
    bands = krev.shape[0]
    rows = bands * K
    full = lambda a: pl.BlockSpec(a.shape, lambda i: (0, 0))
    outs = (
        jax.ShapeDtypeStruct((K, pixels + 2 * LB), jnp.float32),
        jax.ShapeDtypeStruct((rows, channels), jnp.float32),
        jax.ShapeDtypeStruct((rows, LB), jnp.float32),
    )
    return pl.pallas_call(
        functools.partial(sweep_kernel, bands, tile),
        grid=(pixels // tile,),
        in_specs=[
            full(tp),
            full(krev),
            full(fold),
            pl.BlockSpec((tile, channels), lambda i: (i, 0)),
        ],
        out_specs=[full(o) for o in outs],
        out_shape=outs,
        scratch_shapes=[
            pltpu.VMEM((bands * LB, 2 * LB), jnp.bfloat16),
            pltpu.VMEM((bands * LB, 2 * LB), jnp.bfloat16),
            pltpu.VMEM((2 * rows, channels), jnp.bfloat16),
        ],
        compiler_params=pltpu.CompilerParams(vmem_limit_bytes=50 * 2**20),
        name="sweep",
    )(tp, krev, fold, counts)


def shifts(axis):
    count = lax.axis_size(axis)
    up = [(i, i + 1) for i in range(count - 1)]
    return up, [(j, i) for i, j in up]


def body(counts, templates, spectra, response, psf_shape, widths):
    high = lax.Precision.HIGHEST
    pixels = templates.shape[1]
    channels = counts.shape[1]
    bands = channels // CB
    kernel = kernels(psf_shape, widths)
    kernel_here = lax.dynamic_slice_in_dim(kernel, lax.axis_index("chan") * bands, bands, 0)
    krev = jnp.pad(kernel_here[:, ::-1], ((0, 0), (0, 2 * LB - TAPS)))
    fold = jnp.dot(spectra, response, precision=high)
    own_band = (jnp.arange(bands)[:, None] == jnp.arange(channels)[None, :] // CB).astype(
        jnp.float32
    )
    fold_diag = (own_band[:, None, :] * fold[None]).reshape(bands * K, channels)
    up, down = shifts("pix")
    before = lax.ppermute(templates[:, pixels - HW :], "pix", up)
    after = lax.ppermute(templates[:, :HW], "pix", down)
    tp = jnp.concatenate(
        [before, templates, after, jnp.zeros((K, 2 * LB - 2 * HW), jnp.float32)], axis=1
    )
    ext, num, tot = sweep(tp, krev, fold_diag, counts, min(pixels, 2048))

    numerators = jnp.sum(num.reshape(bands, K, channels) * own_band[:, None, :], axis=0)
    totals = jnp.repeat(jnp.sum(tot, axis=1).reshape(bands, K).T, CB, axis=1)
    both = lax.psum(
        jnp.dot(jnp.concatenate([numerators, totals], axis=0), response.T, precision=high),
        ("pix", "chan"),
    )
    new_spectra = spectra * both[:K] / both[K:]

    whole = pixels * lax.axis_size("pix")
    first = lax.axis_index("pix") * pixels
    spots = jnp.arange(LB, dtype=jnp.int32)
    local = jnp.where(spots < 2 * HW, spots, pixels - LB + spots)
    reach = first + local[None, :] + jnp.arange(TAPS, dtype=jnp.int32)[:, None] - HW
    inside = ((reach >= 0) & (reach < whole)).astype(jnp.float32)
    mass = jnp.dot(kernel_here, inside, precision=high)
    weight = jnp.sum(fold.reshape(K, bands, CB), axis=2)
    den = jnp.dot(weight, mass, precision=high)

    from_left = lax.ppermute(ext[:, pixels + HW : pixels + 2 * HW], "pix", up)
    from_right = lax.ppermute(ext[:, :HW], "pix", down)
    own = ext[:, HW : pixels + HW]
    own = jnp.concatenate(
        [own[:, :HW] + from_left, own[:, HW : pixels - HW], own[:, pixels - HW :] + from_right],
        axis=1,
    )
    own, den = lax.psum((own, den), "chan")
    den_map = jnp.concatenate(
        [
            den[:, :HW],
            jnp.broadcast_to(den[:, HW : HW + 1], (K, pixels - 2 * HW)),
            den[:, LB - HW :],
        ],
        axis=1,
    )
    new_templates = templates * own / den_map
    return (new_templates, new_spectra)


def solution(mesh):
    in_specs = (P("pix", "chan"), P(None, "pix"), P(), P(None, "chan"), P(), P())
    out_specs = (P(None, "pix"), P())
    return jax.shard_map(body, mesh=mesh, in_specs=in_specs, out_specs=out_specs, check_vma=False)
```

```python
import functools

import jax
import jax.numpy as jnp
from jax import lax
from jax.experimental import pallas as pl
from jax.experimental.pallas import tpu as pltpu
from jax.sharding import PartitionSpec as P

K = 16
CB = 32
HW = 32
TAPS = 65
LB = 128


def kernels(psf_shape, widths):
    offsets = jnp.arange(TAPS, dtype=jnp.int32) - HW
    in_band = jnp.abs(offsets)[None, :] <= widths[:, None]
    unscaled = jnp.where(in_band, psf_shape, jnp.float32(0.0))
    return unscaled / jnp.sum(unscaled, axis=1, keepdims=True)


def split(x):
    hi = x.astype(jnp.bfloat16)
    lo = (x - hi.astype(jnp.float32)).astype(jnp.bfloat16)
    return hi, lo


def dot(a, b, contract):
    return lax.dot_general(a, b, (contract, ((), ())), preferred_element_type=jnp.float32)


def dot3(a, b, contract):
    rows = a[0].shape[0]
    both = dot(jnp.concatenate([a[0], a[1]], axis=0), b[0], contract)
    return both[:rows] + both[rows:] + dot(a[0], b[1], contract)


def sweep_kernel(bands, tile, tp_ref, krev_ref, fold_ref, counts_ref, ext_ref, num_ref, tot_ref,
                 bhi, blo, fhl):
    step = pl.program_id(0)
    blocks = tile // LB
    rows = bands * K

    @pl.when(step == 0)
    def _():
        for b in range(bands):
            grid = jnp.broadcast_to(krev_ref[b : b + 1, :], (LB, 2 * LB))
            skew = pltpu.roll(grid, 0, 1, stride=1, stride_axis=0)
            hi, lo = split(skew)
            bhi[b * LB : (b + 1) * LB, :] = hi
            blo[b * LB : (b + 1) * LB, :] = lo
        fhi, flo = split(fold_ref[...])
        fhl[0:rows, :] = fhi
        fhl[rows : 2 * rows, :] = flo
        ext_ref[...] = jnp.zeros_like(ext_ref)
        num_ref[...] = jnp.zeros_like(num_ref)
        tot_ref[...] = jnp.zeros_like(tot_ref)

    at = pl.multiple_of(step * tile, tile)
    strip = tp_ref[:, pl.ds(at, tile + LB)]
    win = jnp.concatenate([strip[:, n * LB : (n + 2) * LB] for n in range(blocks)], axis=0)
    blur = dot3(split(win), (bhi[...], blo[...]), ((1,), (1,)))
    x = jnp.concatenate(
        [
            jnp.concatenate(
                [blur[n * K : (n + 1) * K, b * LB : (b + 1) * LB] for n in range(blocks)], axis=1
            )
            for b in range(bands)
        ],
        axis=0,
    )
    tot = x[:, 0:LB]
    for n in range(1, blocks):
        tot = tot + x[:, n * LB : (n + 1) * LB]
    tot_ref[...] += tot
    xs = split(x)
    fhi = fhl[0:rows, :]
    flo = fhl[rows : 2 * rows, :]
    xt = jnp.concatenate([xs[0], xs[1]], axis=0)
    predicted = dot(xt, jnp.concatenate([fhi, fhi], axis=0), ((0,), (0,))) + dot(
        xs[0], flo, ((0,), (0,))
    )
    ratios = split(counts_ref[...].astype(jnp.float32) / predicted)
    num_ref[...] += dot3(xs, ratios, ((1,), (0,)))
    back = dot3((fhi, flo), ratios, ((1,), (1,)))
    rearranged = jnp.concatenate(
        [
            jnp.concatenate(
                [back[b * K : (b + 1) * K, n * LB : (n + 1) * LB] for b in range(bands)], axis=1
            )
            for n in range(blocks)
        ],
        axis=0,
    )
    spread = dot3(split(rearranged), (bhi[...], blo[...]), ((1,), (0,)))
    pieces = []
    for n in range(blocks + 1):
        left = spread[n * K : (n + 1) * K, 0:LB] if n < blocks else None
        right = spread[(n - 1) * K : n * K, LB : 2 * LB] if n > 0 else None
        pieces.append(left if right is None else right if left is None else left + right)
    ext_ref[:, pl.ds(at, tile + LB)] += jnp.concatenate(pieces, axis=1)


def sweep(tp, krev, fold, counts, tile):
    pixels, channels = counts.shape
    bands = krev.shape[0]
    rows = bands * K
    full = lambda a: pl.BlockSpec(a.shape, lambda i: (0, 0))
    outs = (
        jax.ShapeDtypeStruct((K, pixels + 2 * LB), jnp.float32),
        jax.ShapeDtypeStruct((rows, channels), jnp.float32),
        jax.ShapeDtypeStruct((rows, LB), jnp.float32),
    )
    return pl.pallas_call(
        functools.partial(sweep_kernel, bands, tile),
        grid=(pixels // tile,),
        in_specs=[
            full(tp),
            full(krev),
            full(fold),
            pl.BlockSpec((tile, channels), lambda i: (i, 0)),
        ],
        out_specs=[full(o) for o in outs],
        out_shape=outs,
        scratch_shapes=[
            pltpu.VMEM((bands * LB, 2 * LB), jnp.bfloat16),
            pltpu.VMEM((bands * LB, 2 * LB), jnp.bfloat16),
            pltpu.VMEM((2 * rows, channels), jnp.bfloat16),
        ],
        compiler_params=pltpu.CompilerParams(vmem_limit_bytes=50 * 2**20),
        name="sweep",
    )(tp, krev, fold, counts)


def remote(src, dst, sems, slot, axis, to):
    return pltpu.make_async_remote_copy(
        src_ref=src,
        dst_ref=dst,
        send_sem=sems.at[0, slot],
        recv_sem=sems.at[1, slot],
        device_id={axis: to},
        device_id_type=pl.DeviceIdType.MESH,
    )


def exchange_kernel(np_, nc, own_ref, spec_ref, den_ref, resp_ref, map_ref, sum_ref,
                    map_slots, spec_slots, part_slots, map_sems, gather_sems, spec_sems, part_sems):
    ip = lax.axis_index("pix")
    ic = lax.axis_index("chan")
    share = own_ref.shape[1] // nc
    channels = resp_ref.shape[0]
    barrier = pltpu.get_barrier_semaphore()
    for s in range(1, np_):
        pl.semaphore_signal(barrier, inc=1, device_id={"pix": lax.rem(ip + s, np_)},
                            device_id_type=pl.DeviceIdType.MESH)
    for s in range(1, nc):
        pl.semaphore_signal(barrier, inc=1, device_id={"chan": lax.rem(ic + s, nc)},
                            device_id_type=pl.DeviceIdType.MESH)
    pl.semaphore_wait(barrier, np_ + nc - 2)

    def piece(i):
        return pl.ds(pl.multiple_of(i * share, share), share)

    spec_copies = [
        remote(spec_ref, spec_slots.at[ip], spec_sems, s - 1, "pix", lax.rem(ip + s, np_))
        for s in range(1, np_)
    ]
    map_copies = []
    for s in range(1, nc):
        to = lax.rem(ic + s, nc)
        map_copies.append(
            remote(own_ref.at[:, piece(to)], map_slots.at[s - 1], map_sems, s - 1, "chan", to)
        )
    for c in spec_copies + map_copies:
        c.start()
    spec_slots[ip] = spec_ref[...]
    for c in spec_copies:
        c.wait_recv()
    spec = spec_slots[0]
    for i in range(1, np_):
        spec = spec + spec_slots[i]
    part_slots[ic, :, 0:channels] = dot3(split(spec), split(resp_ref[...]), ((1,), (1,)))
    part_slots[ic, :, channels : channels + LB] = den_ref[...]
    part_copies = [
        remote(part_slots.at[ic], part_slots.at[ic], part_sems, s - 1, "chan", lax.rem(ic + s, nc))
        for s in range(1, nc)
    ]
    for c in part_copies:
        c.start()
    for c in map_copies:
        c.wait_recv()
    mine = own_ref[:, piece(ic)]
    for s in range(nc - 1):
        mine = mine + map_slots[s]
    map_ref[:, piece(ic)] = mine
    gathers = [
        remote(map_ref.at[:, piece(ic)], map_ref.at[:, piece(ic)], gather_sems, s - 1, "chan",
               lax.rem(ic + s, nc))
        for s in range(1, nc)
    ]
    for c in gathers:
        c.start()
    for c in part_copies:
        c.wait_recv()
    total = part_slots[0]
    for i in range(1, nc):
        total = total + part_slots[i]
    sum_ref[...] = total
    for c in gathers:
        c.wait_recv()
    for c in spec_copies + map_copies + part_copies + gathers:
        c.wait_send()


def exchange(own, spec, den, response):
    np_, nc = lax.axis_size("pix"), lax.axis_size("chan")
    width = response.shape[0] + LB
    vmem = pl.BlockSpec(memory_space=pltpu.VMEM)
    sems = lambda n: pltpu.SemaphoreType.DMA((2, n))
    return pl.pallas_call(
        functools.partial(exchange_kernel, np_, nc),
        in_specs=[vmem] * 4,
        out_specs=[vmem] * 2,
        out_shape=(
            jax.ShapeDtypeStruct(own.shape, jnp.float32),
            jax.ShapeDtypeStruct((2 * K, width), jnp.float32),
        ),
        scratch_shapes=[
            pltpu.VMEM((nc - 1, K, own.shape[1] // nc), jnp.float32),
            pltpu.VMEM((np_,) + spec.shape, jnp.float32),
            pltpu.VMEM((nc, 2 * K, width), jnp.float32),
            sems(nc - 1),
            sems(nc - 1),
            sems(np_ - 1),
            sems(nc - 1),
        ],
        compiler_params=pltpu.CompilerParams(
            collective_id=0, has_side_effects=True, vmem_limit_bytes=40 * 2**20
        ),
        name="exchange",
    )(own, spec, den, response)


def shifts(axis):
    count = lax.axis_size(axis)
    up = [(i, i + 1) for i in range(count - 1)]
    return up, [(j, i) for i, j in up]


def body(counts, templates, spectra, response, psf_shape, widths):
    high = lax.Precision.HIGHEST
    pixels = templates.shape[1]
    channels = counts.shape[1]
    bands = channels // CB
    kernel = kernels(psf_shape, widths)
    kernel_here = lax.dynamic_slice_in_dim(kernel, lax.axis_index("chan") * bands, bands, 0)
    krev = jnp.pad(kernel_here[:, ::-1], ((0, 0), (0, 2 * LB - TAPS)))
    fold = jnp.dot(spectra, response, precision=high)
    own_band = (jnp.arange(bands)[:, None] == jnp.arange(channels)[None, :] // CB).astype(
        jnp.float32
    )
    fold_diag = (own_band[:, None, :] * fold[None]).reshape(bands * K, channels)
    up, down = shifts("pix")
    before = lax.ppermute(templates[:, pixels - HW :], "pix", up)
    after = lax.ppermute(templates[:, :HW], "pix", down)
    tp = jnp.concatenate(
        [before, templates, after, jnp.zeros((K, 2 * LB - 2 * HW), jnp.float32)], axis=1
    )
    ext, num, tot = sweep(tp, krev, fold_diag, counts, min(pixels, 2048))

    numerators = jnp.sum(num.reshape(bands, K, channels) * own_band[:, None, :], axis=0)
    totals = jnp.repeat(jnp.sum(tot, axis=1).reshape(bands, K).T, CB, axis=1)
    whole = pixels * lax.axis_size("pix")
    first = lax.axis_index("pix") * pixels
    spots = jnp.arange(LB, dtype=jnp.int32)
    local = jnp.where(spots < 2 * HW, spots, pixels - LB + spots)
    reach = first + local[None, :] + jnp.arange(TAPS, dtype=jnp.int32)[:, None] - HW
    inside = ((reach >= 0) & (reach < whole)).astype(jnp.float32)
    mass = jnp.dot(kernel_here, inside, precision=high)
    weight = jnp.sum(fold.reshape(K, bands, CB), axis=2)
    den = jnp.dot(weight, mass, precision=high)

    from_left = lax.ppermute(ext[:, pixels + HW : pixels + 2 * HW], "pix", up)
    from_right = lax.ppermute(ext[:, :HW], "pix", down)
    own = ext[:, HW : pixels + HW]
    own = jnp.concatenate(
        [own[:, :HW] + from_left, own[:, HW : pixels - HW], own[:, pixels - HW :] + from_right],
        axis=1,
    )
    own, both = exchange(
        own,
        jnp.concatenate([numerators, totals], axis=0),
        jnp.pad(den, ((0, K), (0, 0))),
        response,
    )
    channels_all = response.shape[0]
    new_spectra = spectra * both[:K, :channels_all] / both[K:, :channels_all]
    den = both[:K, channels_all:]
    den_map = jnp.concatenate(
        [
            den[:, :HW],
            jnp.broadcast_to(den[:, HW : HW + 1], (K, pixels - 2 * HW)),
            den[:, LB - HW :],
        ],
        axis=1,
    )
    new_templates = templates * own / den_map
    return (new_templates, new_spectra)


def solution(mesh):
    in_specs = (P("pix", "chan"), P(None, "pix"), P(), P(None, "chan"), P(), P())
    out_specs = (P(None, "pix"), P())
    return jax.shard_map(body, mesh=mesh, in_specs=in_specs, out_specs=out_specs, check_vma=False)
```

```python
import functools

import jax
import jax.numpy as jnp
from jax import lax
from jax.experimental import pallas as pl
from jax.experimental.pallas import tpu as pltpu
from jax.sharding import PartitionSpec as P

K = 16
CB = 32
HW = 32
TAPS = 65
LB = 128


def kernels(psf_shape, widths):
    offsets = jnp.arange(TAPS, dtype=jnp.int32) - HW
    in_band = jnp.abs(offsets)[None, :] <= widths[:, None]
    unscaled = jnp.where(in_band, psf_shape, jnp.float32(0.0))
    return unscaled / jnp.sum(unscaled, axis=1, keepdims=True)


def split(x):
    hi = x.astype(jnp.bfloat16)
    lo = (x - hi.astype(jnp.float32)).astype(jnp.bfloat16)
    return hi, lo


def dot(a, b, contract):
    return lax.dot_general(a, b, (contract, ((), ())), preferred_element_type=jnp.float32)


def dot3(a, b, contract):
    rows = a[0].shape[0]
    both = dot(jnp.concatenate([a[0], a[1]], axis=0), b[0], contract)
    return both[:rows] + both[rows:] + dot(a[0], b[1], contract)


def sweep_kernel(bands, tile, tp_ref, krev_ref, fold_ref, counts_ref, ext_ref, num_ref, tot_ref,
                 bhi, blo, fhl):
    step = pl.program_id(0)
    blocks = tile // LB
    rows = bands * K

    @pl.when(step == 0)
    def _():
        for b in range(bands):
            grid = jnp.broadcast_to(krev_ref[b : b + 1, :], (LB, 2 * LB))
            skew = pltpu.roll(grid, 0, 1, stride=1, stride_axis=0)
            hi, lo = split(skew)
            bhi[b * LB : (b + 1) * LB, :] = hi
            blo[b * LB : (b + 1) * LB, :] = lo
        fhi, flo = split(fold_ref[...])
        fhl[0:rows, :] = fhi
        fhl[rows : 2 * rows, :] = flo
        ext_ref[...] = jnp.zeros_like(ext_ref)
        num_ref[...] = jnp.zeros_like(num_ref)
        tot_ref[...] = jnp.zeros_like(tot_ref)

    at = pl.multiple_of(step * tile, tile)
    strip = tp_ref[:, pl.ds(at, tile + LB)]
    win = jnp.concatenate([strip[:, n * LB : (n + 2) * LB] for n in range(blocks)], axis=0)
    blur = dot3(split(win), (bhi[...], blo[...]), ((1,), (1,)))
    x = jnp.concatenate(
        [
            jnp.concatenate(
                [blur[n * K : (n + 1) * K, b * LB : (b + 1) * LB] for n in range(blocks)], axis=1
            )
            for b in range(bands)
        ],
        axis=0,
    )
    tot = x[:, 0:LB]
    for n in range(1, blocks):
        tot = tot + x[:, n * LB : (n + 1) * LB]
    tot_ref[...] += tot
    xs = split(x)
    fhi = fhl[0:rows, :]
    flo = fhl[rows : 2 * rows, :]
    xt = jnp.concatenate([xs[0], xs[1]], axis=0)
    predicted = dot(xt, jnp.concatenate([fhi, fhi], axis=0), ((0,), (0,))) + dot(
        xs[0], flo, ((0,), (0,))
    )
    ratios = split(counts_ref[...].astype(jnp.float32) / predicted)
    num_ref[...] += dot3(xs, ratios, ((1,), (0,)))
    back = dot3((fhi, flo), ratios, ((1,), (1,)))
    rearranged = jnp.concatenate(
        [
            jnp.concatenate(
                [back[b * K : (b + 1) * K, n * LB : (n + 1) * LB] for b in range(bands)], axis=1
            )
            for n in range(blocks)
        ],
        axis=0,
    )
    spread = dot3(split(rearranged), (bhi[...], blo[...]), ((1,), (0,)))
    pieces = []
    for n in range(blocks + 1):
        left = spread[n * K : (n + 1) * K, 0:LB] if n < blocks else None
        right = spread[(n - 1) * K : n * K, LB : 2 * LB] if n > 0 else None
        pieces.append(left if right is None else right if left is None else left + right)
    ext_ref[:, pl.ds(at, tile + LB)] += jnp.concatenate(pieces, axis=1)


def sweep(tp, krev, fold, counts, tile):
    pixels, channels = counts.shape
    bands = krev.shape[0]
    rows = bands * K
    full = lambda a: pl.BlockSpec(a.shape, lambda i: (0, 0))
    outs = (
        jax.ShapeDtypeStruct((K, pixels + 2 * LB), jnp.float32),
        jax.ShapeDtypeStruct((rows, channels), jnp.float32),
        jax.ShapeDtypeStruct((rows, LB), jnp.float32),
    )
    return pl.pallas_call(
        functools.partial(sweep_kernel, bands, tile),
        grid=(pixels // tile,),
        in_specs=[
            full(tp),
            full(krev),
            full(fold),
            pl.BlockSpec((tile, channels), lambda i: (i, 0)),
        ],
        out_specs=[full(o) for o in outs],
        out_shape=outs,
        scratch_shapes=[
            pltpu.VMEM((bands * LB, 2 * LB), jnp.bfloat16),
            pltpu.VMEM((bands * LB, 2 * LB), jnp.bfloat16),
            pltpu.VMEM((2 * rows, channels), jnp.bfloat16),
        ],
        compiler_params=pltpu.CompilerParams(vmem_limit_bytes=50 * 2**20),
        name="sweep",
    )(tp, krev, fold, counts)


def remote(src, dst, sems, slot, axis, to):
    return pltpu.make_async_remote_copy(
        src_ref=src,
        dst_ref=dst,
        send_sem=sems.at[0, slot],
        recv_sem=sems.at[1, slot],
        device_id={axis: to},
        device_id_type=pl.DeviceIdType.MESH,
    )


def exchange_kernel(np_, nc, ext_ref, spec_ref, den_ref, resp_ref, map_ref, sum_ref,
                    own_ref, edge_slots, map_slots, spec_slots, part_slots, edge_sems, map_sems,
                    gather_sems, spec_sems, part_sems):
    ip = lax.axis_index("pix")
    ic = lax.axis_index("chan")
    share = own_ref.shape[1] // nc
    channels = resp_ref.shape[0]
    barrier = pltpu.get_barrier_semaphore()
    for s in range(1, np_):
        pl.semaphore_signal(barrier, inc=1, device_id={"pix": lax.rem(ip + s, np_)},
                            device_id_type=pl.DeviceIdType.MESH)
    for s in range(1, nc):
        pl.semaphore_signal(barrier, inc=1, device_id={"chan": lax.rem(ic + s, nc)},
                            device_id_type=pl.DeviceIdType.MESH)
    pl.semaphore_wait(barrier, np_ + nc - 2)

    def piece(i):
        return pl.ds(pl.multiple_of(i * share, share), share)

    pixels = own_ref.shape[1]
    edge_copies = [
        remote(ext_ref.at[:, 0:LB], edge_slots.at[0], edge_sems, 0, "pix",
               lax.rem(ip + np_ - 1, np_)),
        remote(ext_ref.at[:, pixels : pixels + LB], edge_slots.at[1], edge_sems, 1, "pix",
               lax.rem(ip + 1, np_)),
    ]
    for c in edge_copies:
        c.start()
    spec_copies = [
        remote(spec_ref, spec_slots.at[ip], spec_sems, s - 1, "pix", lax.rem(ip + s, np_))
        for s in range(1, np_)
    ]
    map_copies = []
    for s in range(1, nc):
        to = lax.rem(ic + s, nc)
        map_copies.append(
            remote(own_ref.at[:, piece(to)], map_slots.at[s - 1], map_sems, s - 1, "chan", to)
        )
    for c in spec_copies:
        c.start()
    own_ref[...] = ext_ref[:, HW : pixels + HW]
    for c in edge_copies:
        c.wait_recv()
    has_left = jnp.where(ip > 0, 1.0, 0.0).astype(jnp.float32)
    has_right = jnp.where(ip < np_ - 1, 1.0, 0.0).astype(jnp.float32)
    own_ref[:, 0:HW] += edge_slots[1][:, HW : 2 * HW] * has_left
    own_ref[:, pixels - HW : pixels] += edge_slots[0][:, 0:HW] * has_right
    for c in map_copies:
        c.start()
    spec_slots[ip] = spec_ref[...]
    for c in spec_copies:
        c.wait_recv()
    spec = spec_slots[0]
    for i in range(1, np_):
        spec = spec + spec_slots[i]
    part_slots[ic, :, 0:channels] = dot3(split(spec), split(resp_ref[...]), ((1,), (1,)))
    part_slots[ic, :, channels : channels + LB] = den_ref[...]
    part_copies = [
        remote(part_slots.at[ic], part_slots.at[ic], part_sems, s - 1, "chan", lax.rem(ic + s, nc))
        for s in range(1, nc)
    ]
    for c in part_copies:
        c.start()
    for c in map_copies:
        c.wait_recv()
    mine = own_ref[:, piece(ic)]
    for s in range(nc - 1):
        mine = mine + map_slots[s]
    map_ref[:, piece(ic)] = mine
    gathers = [
        remote(map_ref.at[:, piece(ic)], map_ref.at[:, piece(ic)], gather_sems, s - 1, "chan",
               lax.rem(ic + s, nc))
        for s in range(1, nc)
    ]
    for c in gathers:
        c.start()
    for c in part_copies:
        c.wait_recv()
    total = part_slots[0]
    for i in range(1, nc):
        total = total + part_slots[i]
    sum_ref[...] = total
    for c in gathers:
        c.wait_recv()
    for c in edge_copies + spec_copies + map_copies + part_copies + gathers:
        c.wait_send()


def exchange(ext, spec, den, response):
    shape = (K, ext.shape[1] - 2 * LB)
    np_, nc = lax.axis_size("pix"), lax.axis_size("chan")
    width = response.shape[0] + LB
    vmem = pl.BlockSpec(memory_space=pltpu.VMEM)
    sems = lambda n: pltpu.SemaphoreType.DMA((2, n))
    return pl.pallas_call(
        functools.partial(exchange_kernel, np_, nc),
        in_specs=[vmem] * 4,
        out_specs=[vmem] * 2,
        out_shape=(
            jax.ShapeDtypeStruct(shape, jnp.float32),
            jax.ShapeDtypeStruct((2 * K, width), jnp.float32),
        ),
        scratch_shapes=[
            pltpu.VMEM(shape, jnp.float32),
            pltpu.VMEM((2, K, LB), jnp.float32),
            pltpu.VMEM((nc - 1, K, shape[1] // nc), jnp.float32),
            pltpu.VMEM((np_,) + spec.shape, jnp.float32),
            pltpu.VMEM((nc, 2 * K, width), jnp.float32),
            sems(2),
            sems(nc - 1),
            sems(nc - 1),
            sems(np_ - 1),
            sems(nc - 1),
        ],
        compiler_params=pltpu.CompilerParams(
            collective_id=0, has_side_effects=True, vmem_limit_bytes=40 * 2**20
        ),
        name="exchange",
    )(ext, spec, den, response)


def shifts(axis):
    count = lax.axis_size(axis)
    up = [(i, i + 1) for i in range(count - 1)]
    return up, [(j, i) for i, j in up]


def body(counts, templates, spectra, response, psf_shape, widths):
    high = lax.Precision.HIGHEST
    pixels = templates.shape[1]
    channels = counts.shape[1]
    bands = channels // CB
    kernel = kernels(psf_shape, widths)
    kernel_here = lax.dynamic_slice_in_dim(kernel, lax.axis_index("chan") * bands, bands, 0)
    krev = jnp.pad(kernel_here[:, ::-1], ((0, 0), (0, 2 * LB - TAPS)))
    fold = jnp.dot(spectra, response, precision=high)
    own_band = (jnp.arange(bands)[:, None] == jnp.arange(channels)[None, :] // CB).astype(
        jnp.float32
    )
    fold_diag = (own_band[:, None, :] * fold[None]).reshape(bands * K, channels)
    up, down = shifts("pix")
    before = lax.ppermute(templates[:, pixels - HW :], "pix", up)
    after = lax.ppermute(templates[:, :HW], "pix", down)
    tp = jnp.concatenate(
        [before, templates, after, jnp.zeros((K, 2 * LB - 2 * HW), jnp.float32)], axis=1
    )
    ext, num, tot = sweep(tp, krev, fold_diag, counts, min(pixels, 2048))

    numerators = jnp.sum(num.reshape(bands, K, channels) * own_band[:, None, :], axis=0)
    totals = jnp.repeat(jnp.sum(tot, axis=1).reshape(bands, K).T, CB, axis=1)
    whole = pixels * lax.axis_size("pix")
    first = lax.axis_index("pix") * pixels
    spots = jnp.arange(LB, dtype=jnp.int32)
    local = jnp.where(spots < 2 * HW, spots, pixels - LB + spots)
    reach = first + local[None, :] + jnp.arange(TAPS, dtype=jnp.int32)[:, None] - HW
    inside = ((reach >= 0) & (reach < whole)).astype(jnp.float32)
    mass = jnp.dot(kernel_here, inside, precision=high)
    weight = jnp.sum(fold.reshape(K, bands, CB), axis=2)
    den = jnp.dot(weight, mass, precision=high)

    own, both = exchange(
        ext,
        jnp.concatenate([numerators, totals], axis=0),
        jnp.pad(den, ((0, K), (0, 0))),
        response,
    )
    channels_all = response.shape[0]
    new_spectra = spectra * both[:K, :channels_all] / both[K:, :channels_all]
    den = both[:K, channels_all:]
    den_map = jnp.concatenate(
        [
            den[:, :HW],
            jnp.broadcast_to(den[:, HW : HW + 1], (K, pixels - 2 * HW)),
            den[:, LB - HW :],
        ],
        axis=1,
    )
    new_templates = templates * own / den_map
    return (new_templates, new_spectra)


def solution(mesh):
    in_specs = (P("pix", "chan"), P(None, "pix"), P(), P(None, "chan"), P(), P())
    out_specs = (P(None, "pix"), P())
    return jax.shard_map(body, mesh=mesh, in_specs=in_specs, out_specs=out_specs, check_vma=False)
```

```python
import functools

import jax
import jax.numpy as jnp
from jax import lax
from jax.experimental import pallas as pl
from jax.experimental.pallas import tpu as pltpu
from jax.sharding import PartitionSpec as P

K = 16
CB = 32
HW = 32
TAPS = 65
LB = 128


def kernels(psf_shape, widths):
    offsets = jnp.arange(TAPS, dtype=jnp.int32) - HW
    in_band = jnp.abs(offsets)[None, :] <= widths[:, None]
    unscaled = jnp.where(in_band, psf_shape, jnp.float32(0.0))
    return unscaled / jnp.sum(unscaled, axis=1, keepdims=True)


def split(x):
    hi = x.astype(jnp.bfloat16)
    lo = (x - hi.astype(jnp.float32)).astype(jnp.bfloat16)
    return hi, lo


def dot(a, b, contract):
    return lax.dot_general(a, b, (contract, ((), ())), preferred_element_type=jnp.float32)


def dot3(a, b, contract):
    rows = a[0].shape[0]
    both = dot(jnp.concatenate([a[0], a[1]], axis=0), b[0], contract)
    return both[:rows] + both[rows:] + dot(a[0], b[1], contract)


def sweep_kernel(bands, tile, tp_ref, krev_ref, fold_ref, counts_ref, ext_ref, num_ref, tot_ref,
                 bhi, blo, fhl):
    step = pl.program_id(0)
    blocks = tile // LB
    rows = bands * K

    @pl.when(step == 0)
    def _():
        for b in range(bands):
            grid = jnp.broadcast_to(krev_ref[b : b + 1, :], (LB, 2 * LB))
            skew = pltpu.roll(grid, 0, 1, stride=1, stride_axis=0)
            hi, lo = split(skew)
            bhi[b * LB : (b + 1) * LB, :] = hi
            blo[b * LB : (b + 1) * LB, :] = lo
        fhi, flo = split(fold_ref[...])
        fhl[0:rows, :] = fhi
        fhl[rows : 2 * rows, :] = flo
        ext_ref[...] = jnp.zeros_like(ext_ref)
        num_ref[...] = jnp.zeros_like(num_ref)
        tot_ref[...] = jnp.zeros_like(tot_ref)

    at = pl.multiple_of(step * tile, tile)
    strip = tp_ref[:, pl.ds(at, tile + LB)]
    win = jnp.concatenate([strip[:, n * LB : (n + 2) * LB] for n in range(blocks)], axis=0)
    blur = dot3(split(win), (bhi[...], blo[...]), ((1,), (1,)))
    x = jnp.concatenate(
        [
            jnp.concatenate(
                [blur[n * K : (n + 1) * K, b * LB : (b + 1) * LB] for n in range(blocks)], axis=1
            )
            for b in range(bands)
        ],
        axis=0,
    )
    tot = x[:, 0:LB]
    for n in range(1, blocks):
        tot = tot + x[:, n * LB : (n + 1) * LB]
    tot_ref[...] += tot
    xs = split(x)
    fhi = fhl[0:rows, :]
    flo = fhl[rows : 2 * rows, :]
    xt = jnp.concatenate([xs[0], xs[1]], axis=0)
    predicted = dot(xt, jnp.concatenate([fhi, fhi], axis=0), ((0,), (0,))) + dot(
        xs[0], flo, ((0,), (0,))
    )
    ratios = split(counts_ref[...].astype(jnp.float32) / predicted)
    num_ref[...] += dot3(xs, ratios, ((1,), (0,)))
    back = dot3((fhi, flo), ratios, ((1,), (1,)))
    rearranged = jnp.concatenate(
        [
            jnp.concatenate(
                [back[b * K : (b + 1) * K, n * LB : (n + 1) * LB] for b in range(bands)], axis=1
            )
            for n in range(blocks)
        ],
        axis=0,
    )
    spread = dot3(split(rearranged), (bhi[...], blo[...]), ((1,), (0,)))
    pieces = []
    for n in range(blocks + 1):
        left = spread[n * K : (n + 1) * K, 0:LB] if n < blocks else None
        right = spread[(n - 1) * K : n * K, LB : 2 * LB] if n > 0 else None
        pieces.append(left if right is None else right if left is None else left + right)
    ext_ref[:, pl.ds(at, tile + LB)] += jnp.concatenate(pieces, axis=1)


def sweep(tp, krev, fold, counts, tile):
    pixels, channels = counts.shape
    bands = krev.shape[0]
    rows = bands * K
    full = lambda a: pl.BlockSpec(a.shape, lambda i: (0, 0))
    outs = (
        jax.ShapeDtypeStruct((K, pixels + 2 * LB), jnp.float32),
        jax.ShapeDtypeStruct((rows, channels), jnp.float32),
        jax.ShapeDtypeStruct((rows, LB), jnp.float32),
    )
    return pl.pallas_call(
        functools.partial(sweep_kernel, bands, tile),
        grid=(pixels // tile,),
        in_specs=[
            full(tp),
            full(krev),
            full(fold),
            pl.BlockSpec((tile, channels), lambda i: (i, 0)),
        ],
        out_specs=[full(o) for o in outs],
        out_shape=outs,
        scratch_shapes=[
            pltpu.VMEM((bands * LB, 2 * LB), jnp.bfloat16),
            pltpu.VMEM((bands * LB, 2 * LB), jnp.bfloat16),
            pltpu.VMEM((2 * rows, channels), jnp.bfloat16),
        ],
        compiler_params=pltpu.CompilerParams(vmem_limit_bytes=50 * 2**20),
        name="sweep",
    )(tp, krev, fold, counts)


def remote(src, dst, sems, slot, axis, to):
    return pltpu.make_async_remote_copy(
        src_ref=src,
        dst_ref=dst,
        send_sem=sems.at[0, slot],
        recv_sem=sems.at[1, slot],
        device_id={axis: to},
        device_id_type=pl.DeviceIdType.MESH,
    )


def exchange_kernel(np_, nc, chunks, ext_ref, spec_ref, den_ref, resp_ref, map_ref, sum_ref,
                    dsum_ref, own_ref, edge_slots, in_slots, mid_slots, spec_slots, part_slots,
                    den_slots, edge_sems, in_sems, mid_sems, out_sems, spec_sems, part_sems,
                    den_sems, sum_sems):
    ip = lax.axis_index("pix")
    ic = lax.axis_index("chan")
    pixels = own_ref.shape[1]
    width = pixels // chunks
    lines = resp_ref.shape[0] // np_
    half = nc // 2
    side = lax.div(ic, half)
    inner = ic + 1 - 2 * side
    outer = lax.rem(ic - 1 + 2 * side + nc, nc)
    depth = (half - 1 - ic) * (1 - side) + (ic - half) * side
    barrier = pltpu.get_barrier_semaphore()
    for s in range(1, np_):
        pl.semaphore_signal(barrier, inc=1, device_id={"pix": lax.rem(ip + s, np_)},
                            device_id_type=pl.DeviceIdType.MESH)
    for s in range(1, nc):
        pl.semaphore_signal(barrier, inc=1, device_id={"chan": lax.rem(ic + s, nc)},
                            device_id_type=pl.DeviceIdType.MESH)
    pl.semaphore_wait(barrier, np_ + nc - 2)

    edge_copies = [
        remote(ext_ref.at[:, 0:LB], edge_slots.at[0], edge_sems, 0, "pix",
               lax.rem(ip + np_ - 1, np_)),
        remote(ext_ref.at[:, pixels : pixels + LB], edge_slots.at[1], edge_sems, 1, "pix",
               lax.rem(ip + 1, np_)),
    ]
    spec_copies = [
        remote(spec_ref, spec_slots.at[ip], spec_sems, s - 1, "pix", lax.rem(ip + s, np_))
        for s in range(1, np_)
    ]
    den_copies = [
        remote(den_ref, den_slots.at[ic], den_sems, s - 1, "chan", lax.rem(ic + s, nc))
        for s in range(1, nc)
    ]
    part_copies = [
        remote(part_slots.at[ic], part_slots.at[ic], part_sems, s - 1, "chan", lax.rem(ic + s, nc))
        for s in range(1, nc)
    ]
    sum_copies = [
        remote(sum_ref.at[ip], sum_ref.at[ip], sum_sems, s - 1, "pix", lax.rem(ip + s, np_))
        for s in range(1, np_)
    ]
    for c in edge_copies + spec_copies + den_copies:
        c.start()
    own_ref[...] = ext_ref[:, HW : pixels + HW]
    spec_slots[ip] = spec_ref[...]
    den_slots[ic] = den_ref[...]
    for c in edge_copies:
        c.wait_recv()
    has_left = jnp.where(ip > 0, 1.0, 0.0).astype(jnp.float32)
    has_right = jnp.where(ip < np_ - 1, 1.0, 0.0).astype(jnp.float32)
    own_ref[:, 0:HW] += edge_slots[1][:, HW : 2 * HW] * has_left
    own_ref[:, pixels - HW : pixels] += edge_slots[0][:, 0:HW] * has_right

    def columns(t):
        return slice(t * width, (t + 1) * width)

    def inward(t):
        return remote(own_ref.at[:, columns(t)], in_slots.at[t], in_sems, t, "chan", inner)

    def swap(t):
        return remote(own_ref.at[:, columns(t)], mid_slots.at[t], mid_sems, t, "chan", inner)

    def outward(t):
        return remote(map_ref.at[:, columns(t)], map_ref.at[:, columns(t)], out_sems, t, "chan",
                      outer)

    def send_in(t):
        @pl.when(depth < half - 1)
        def _():
            inward(t).wait_recv()
            own_ref[:, columns(t)] += in_slots[t]

        @pl.when(depth == 0)
        def _():
            swap(t).start()

        @pl.when(depth > 0)
        def _():
            if t >= 2:
                inward(t - 2).wait_send()
            inward(t).start()

    def send_out(t):
        @pl.when(depth == 0)
        def _():
            swap(t).wait_recv()
            map_ref[:, columns(t)] = own_ref[:, columns(t)] + mid_slots[t]

        @pl.when(depth > 0)
        def _():
            outward(t).wait_recv()

        @pl.when(depth < half - 1)
        def _():
            outward(t).start()

    def spectral_terms():
        for c in spec_copies:
            c.wait_recv()
        spec = spec_slots[0]
        for i in range(1, np_):
            spec = spec + spec_slots[i]
        here = resp_ref[pl.ds(pl.multiple_of(ip * lines, lines), lines), :]
        part_slots[ic] = dot3(split(spec), split(here), ((1,), (1,)))
        for c in part_copies:
            c.start()

    def spectral_sums():
        for c in part_copies + den_copies:
            c.wait_recv()
        total = part_slots[0]
        den = den_slots[0]
        for i in range(1, nc):
            total = total + part_slots[i]
            den = den + den_slots[i]
        sum_ref[ip] = total
        dsum_ref[...] = den
        for c in sum_copies:
            c.start()

    lag = 2
    for t in range(chunks + lag):
        if t < chunks:
            send_in(t)
        if t == 2:
            spectral_terms()
        if t == 5:
            spectral_sums()
        if t >= lag:
            send_out(t - lag)
    for c in sum_copies:
        c.wait_recv()

    @pl.when(depth == 0)
    def _():
        for t in range(chunks):
            swap(t).wait_send()

    @pl.when(depth > 0)
    def _():
        for t in range(chunks - 2, chunks):
            inward(t).wait_send()

    @pl.when(depth < half - 1)
    def _():
        for t in range(chunks):
            outward(t).wait_send()

    for c in edge_copies + spec_copies + den_copies + part_copies + sum_copies:
        c.wait_send()


def exchange(ext, spec, den, response):
    pixels = ext.shape[1] - 2 * LB
    chunks = 8
    np_, nc = lax.axis_size("pix"), lax.axis_size("chan")
    lines = response.shape[0] // np_
    vmem = pl.BlockSpec(memory_space=pltpu.VMEM)
    sems = lambda n: pltpu.SemaphoreType.DMA((2, n))
    box = lambda *shape: pltpu.VMEM(shape, jnp.float32)
    return pl.pallas_call(
        functools.partial(exchange_kernel, np_, nc, chunks),
        in_specs=[vmem] * 4,
        out_specs=[vmem] * 3,
        out_shape=(
            jax.ShapeDtypeStruct((K, pixels), jnp.float32),
            jax.ShapeDtypeStruct((np_, 2 * K, lines), jnp.float32),
            jax.ShapeDtypeStruct(den.shape, jnp.float32),
        ),
        scratch_shapes=[
            box(K, pixels),
            box(2, K, LB),
            box(chunks, K, pixels // chunks),
            box(chunks, K, pixels // chunks),
            box(np_, *spec.shape),
            box(nc, 2 * K, lines),
            box(nc, *den.shape),
            sems(2),
            sems(chunks),
            sems(chunks),
            sems(chunks),
            sems(np_ - 1),
            sems(nc - 1),
            sems(nc - 1),
            sems(np_ - 1),
        ],
        compiler_params=pltpu.CompilerParams(
            collective_id=0, has_side_effects=True, vmem_limit_bytes=40 * 2**20
        ),
        name="exchange",
    )(ext, spec, den, response)


def shifts(axis):
    count = lax.axis_size(axis)
    up = [(i, i + 1) for i in range(count - 1)]
    return up, [(j, i) for i, j in up]


def body(counts, templates, spectra, response, psf_shape, widths):
    high = lax.Precision.HIGHEST
    pixels = templates.shape[1]
    channels = counts.shape[1]
    bands = channels // CB
    kernel = kernels(psf_shape, widths)
    kernel_here = lax.dynamic_slice_in_dim(kernel, lax.axis_index("chan") * bands, bands, 0)
    krev = jnp.pad(kernel_here[:, ::-1], ((0, 0), (0, 2 * LB - TAPS)))
    fold = jnp.dot(spectra, response, precision=high)
    own_band = (jnp.arange(bands)[:, None] == jnp.arange(channels)[None, :] // CB).astype(
        jnp.float32
    )
    fold_diag = (own_band[:, None, :] * fold[None]).reshape(bands * K, channels)
    up, down = shifts("pix")
    before = lax.ppermute(templates[:, pixels - HW :], "pix", up)
    after = lax.ppermute(templates[:, :HW], "pix", down)
    tp = jnp.concatenate(
        [before, templates, after, jnp.zeros((K, 2 * LB - 2 * HW), jnp.float32)], axis=1
    )
    ext, num, tot = sweep(tp, krev, fold_diag, counts, min(pixels, 2048))

    numerators = jnp.sum(num.reshape(bands, K, channels) * own_band[:, None, :], axis=0)
    totals = jnp.repeat(jnp.sum(tot, axis=1).reshape(bands, K).T, CB, axis=1)
    whole = pixels * lax.axis_size("pix")
    first = lax.axis_index("pix") * pixels
    spots = jnp.arange(LB, dtype=jnp.int32)
    local = jnp.where(spots < 2 * HW, spots, pixels - LB + spots)
    reach = first + local[None, :] + jnp.arange(TAPS, dtype=jnp.int32)[:, None] - HW
    inside = ((reach >= 0) & (reach < whole)).astype(jnp.float32)
    mass = jnp.dot(kernel_here, inside, precision=high)
    weight = jnp.sum(fold.reshape(K, bands, CB), axis=2)
    den = jnp.dot(weight, mass, precision=high)

    own, both, den = exchange(
        ext, jnp.concatenate([numerators, totals], axis=0), den, response
    )
    both = jnp.transpose(both, (1, 0, 2)).reshape(2 * K, response.shape[0])
    new_spectra = spectra * both[:K] / both[K:]
    den_map = jnp.concatenate(
        [
            den[:, :HW],
            jnp.broadcast_to(den[:, HW : HW + 1], (K, pixels - 2 * HW)),
            den[:, LB - HW :],
        ],
        axis=1,
    )
    new_templates = templates * own / den_map
    return (new_templates, new_spectra)


def solution(mesh):
    in_specs = (P("pix", "chan"), P(None, "pix"), P(), P(None, "chan"), P(), P())
    out_specs = (P(None, "pix"), P())
    return jax.shard_map(body, mesh=mesh, in_specs=in_specs, out_specs=out_specs, check_vma=False)
```

```python
import functools

import jax
import jax.numpy as jnp
from jax import lax
from jax.experimental import pallas as pl
from jax.experimental.pallas import tpu as pltpu
from jax.sharding import PartitionSpec as P

K = 16
CB = 32
HW = 32
TAPS = 65
LB = 128


def kernels(psf_shape, widths):
    offsets = jnp.arange(TAPS, dtype=jnp.int32) - HW
    in_band = jnp.abs(offsets)[None, :] <= widths[:, None]
    unscaled = jnp.where(in_band, psf_shape, jnp.float32(0.0))
    return unscaled / jnp.sum(unscaled, axis=1, keepdims=True)


def split(x):
    hi = x.astype(jnp.bfloat16)
    lo = (x - hi.astype(jnp.float32)).astype(jnp.bfloat16)
    return hi, lo


def dot(a, b, contract):
    return lax.dot_general(a, b, (contract, ((), ())), preferred_element_type=jnp.float32)


def dot3(a, b, contract):
    rows = a[0].shape[0]
    both = dot(jnp.concatenate([a[0], a[1]], axis=0), b[0], contract)
    return both[:rows] + both[rows:] + dot(a[0], b[1], contract)


def sweep_kernel(bands, tile, tp_ref, krev_ref, fold_ref, counts_ref, ext_ref, num_ref, tot_ref,
                 bhi, blo, fhl):
    step = pl.program_id(0)
    blocks = tile // LB
    rows = bands * K

    @pl.when(step == 0)
    def _():
        for b in range(bands):
            grid = jnp.broadcast_to(krev_ref[b : b + 1, :], (LB, 2 * LB))
            skew = pltpu.roll(grid, 0, 1, stride=1, stride_axis=0)
            hi, lo = split(skew)
            bhi[b * LB : (b + 1) * LB, :] = hi
            blo[b * LB : (b + 1) * LB, :] = lo
        fhi, flo = split(fold_ref[...])
        fhl[0:rows, :] = fhi
        fhl[rows : 2 * rows, :] = flo
        ext_ref[...] = jnp.zeros_like(ext_ref)
        num_ref[...] = jnp.zeros_like(num_ref)
        tot_ref[...] = jnp.zeros_like(tot_ref)

    at = pl.multiple_of(step * tile, tile)
    strip = tp_ref[:, pl.ds(at, tile + LB)]
    win = jnp.concatenate([strip[:, n * LB : (n + 2) * LB] for n in range(blocks)], axis=0)
    blur = dot3(split(win), (bhi[...], blo[...]), ((1,), (1,)))
    x = jnp.concatenate(
        [
            jnp.concatenate(
                [blur[n * K : (n + 1) * K, b * LB : (b + 1) * LB] for n in range(blocks)], axis=1
            )
            for b in range(bands)
        ],
        axis=0,
    )
    tot = x[:, 0:LB]
    for n in range(1, blocks):
        tot = tot + x[:, n * LB : (n + 1) * LB]
    tot_ref[...] += tot
    xs = split(x)
    fhi = fhl[0:rows, :]
    flo = fhl[rows : 2 * rows, :]
    xt = jnp.concatenate([xs[0], xs[1]], axis=0)
    predicted = dot(xt, jnp.concatenate([fhi, fhi], axis=0), ((0,), (0,))) + dot(
        xs[0], flo, ((0,), (0,))
    )
    ratios = split(counts_ref[...].astype(jnp.float32) / predicted)
    num_ref[...] += dot3(xs, ratios, ((1,), (0,)))
    back = dot3((fhi, flo), ratios, ((1,), (1,)))
    rearranged = jnp.concatenate(
        [
            jnp.concatenate(
                [back[b * K : (b + 1) * K, n * LB : (n + 1) * LB] for b in range(bands)], axis=1
            )
            for n in range(blocks)
        ],
        axis=0,
    )
    spread = dot3(split(rearranged), (bhi[...], blo[...]), ((1,), (0,)))
    pieces = []
    for n in range(blocks + 1):
        left = spread[n * K : (n + 1) * K, 0:LB] if n < blocks else None
        right = spread[(n - 1) * K : n * K, LB : 2 * LB] if n > 0 else None
        pieces.append(left if right is None else right if left is None else left + right)
    ext_ref[:, pl.ds(at, tile + LB)] += jnp.concatenate(pieces, axis=1)


def sweep(tp, krev, fold, counts, tile):
    pixels, channels = counts.shape
    bands = krev.shape[0]
    rows = bands * K
    full = lambda a: pl.BlockSpec(a.shape, lambda i: (0, 0))
    outs = (
        jax.ShapeDtypeStruct((K, pixels + 2 * LB), jnp.float32),
        jax.ShapeDtypeStruct((rows, channels), jnp.float32),
        jax.ShapeDtypeStruct((rows, LB), jnp.float32),
    )
    return pl.pallas_call(
        functools.partial(sweep_kernel, bands, tile),
        grid=(pixels // tile,),
        in_specs=[
            full(tp),
            full(krev),
            full(fold),
            pl.BlockSpec((tile, channels), lambda i: (i, 0)),
        ],
        out_specs=[full(o) for o in outs],
        out_shape=outs,
        scratch_shapes=[
            pltpu.VMEM((bands * LB, 2 * LB), jnp.bfloat16),
            pltpu.VMEM((bands * LB, 2 * LB), jnp.bfloat16),
            pltpu.VMEM((2 * rows, channels), jnp.bfloat16),
        ],
        compiler_params=pltpu.CompilerParams(vmem_limit_bytes=50 * 2**20),
        name="sweep",
    )(tp, krev, fold, counts)


def remote(src, dst, sems, slot, axis, to):
    return pltpu.make_async_remote_copy(
        src_ref=src,
        dst_ref=dst,
        send_sem=sems.at[0, slot],
        recv_sem=sems.at[1, slot],
        device_id={axis: to},
        device_id_type=pl.DeviceIdType.MESH,
    )


def exchange_kernel(np_, nc, ext_ref, spec_ref, den_ref, resp_ref, map_ref, sum_ref,
                    dsum_ref, own_ref, edge_slots, map_slots, spec_slots, part_slots,
                    den_slots, edge_sems, map_sems, gather_sems, spec_sems, part_sems,
                    den_sems, sum_sems):
    ip = lax.axis_index("pix")
    ic = lax.axis_index("chan")
    pixels = own_ref.shape[1]
    share = pixels // nc
    lines = resp_ref.shape[0] // np_
    barrier = pltpu.get_barrier_semaphore()
    for s in range(1, np_):
        pl.semaphore_signal(barrier, inc=1, device_id={"pix": lax.rem(ip + s, np_)},
                            device_id_type=pl.DeviceIdType.MESH)
    for s in range(1, nc):
        pl.semaphore_signal(barrier, inc=1, device_id={"chan": lax.rem(ic + s, nc)},
                            device_id_type=pl.DeviceIdType.MESH)
    pl.semaphore_wait(barrier, np_ + nc - 2)

    edge_copies = [
        remote(ext_ref.at[:, 0:LB], edge_slots.at[0], edge_sems, 0, "pix",
               lax.rem(ip + np_ - 1, np_)),
        remote(ext_ref.at[:, pixels : pixels + LB], edge_slots.at[1], edge_sems, 1, "pix",
               lax.rem(ip + 1, np_)),
    ]
    spec_copies = [
        remote(spec_ref, spec_slots.at[ip], spec_sems, s - 1, "pix", lax.rem(ip + s, np_))
        for s in range(1, np_)
    ]
    den_copies = [
        remote(den_ref, den_slots.at[ic], den_sems, s - 1, "chan", lax.rem(ic + s, nc))
        for s in range(1, nc)
    ]
    part_copies = [
        remote(part_slots.at[ic], part_slots.at[ic], part_sems, s - 1, "chan", lax.rem(ic + s, nc))
        for s in range(1, nc)
    ]
    sum_copies = [
        remote(sum_ref.at[ip], sum_ref.at[ip], sum_sems, s - 1, "pix", lax.rem(ip + s, np_))
        for s in range(1, np_)
    ]
    for c in edge_copies + spec_copies + den_copies:
        c.start()
    own_ref[...] = ext_ref[:, HW : pixels + HW]
    spec_slots[ip] = spec_ref[...]
    den_slots[ic] = den_ref[...]
    for c in edge_copies:
        c.wait_recv()
    has_left = jnp.where(ip > 0, 1.0, 0.0).astype(jnp.float32)
    has_right = jnp.where(ip < np_ - 1, 1.0, 0.0).astype(jnp.float32)
    own_ref[:, 0:HW] += edge_slots[1][:, HW : 2 * HW] * has_left
    own_ref[:, pixels - HW : pixels] += edge_slots[0][:, 0:HW] * has_right

    def piece(i):
        return pl.ds(pl.multiple_of(i * share, share), share)

    map_copies = []
    for s in range(1, nc):
        to = lax.rem(ic + s, nc)
        map_copies.append(
            remote(own_ref.at[:, piece(to)], map_slots.at[s - 1], map_sems, s - 1, "chan", to)
        )
    for c in map_copies:
        c.start()

    def spectral_terms():
        for c in spec_copies:
            c.wait_recv()
        spec = spec_slots[0]
        for i in range(1, np_):
            spec = spec + spec_slots[i]
        here = resp_ref[pl.ds(pl.multiple_of(ip * lines, lines), lines), :]
        part_slots[ic] = dot3(split(spec), split(here), ((1,), (1,)))
        for c in part_copies:
            c.start()

    def spectral_sums():
        for c in part_copies + den_copies:
            c.wait_recv()
        total = part_slots[0]
        den = den_slots[0]
        for i in range(1, nc):
            total = total + part_slots[i]
            den = den + den_slots[i]
        sum_ref[ip] = total
        dsum_ref[...] = den
        for c in sum_copies:
            c.start()

    spectral_terms()
    for c in map_copies:
        c.wait_recv()
    mine = own_ref[:, piece(ic)]
    for s in range(nc - 1):
        mine = mine + map_slots[s]
    map_ref[:, piece(ic)] = mine
    gathers = [
        remote(map_ref.at[:, piece(ic)], map_ref.at[:, piece(ic)], gather_sems, s - 1, "chan",
               lax.rem(ic + s, nc))
        for s in range(1, nc)
    ]
    for c in gathers:
        c.start()
    spectral_sums()
    for c in sum_copies + gathers:
        c.wait_recv()
    for c in (edge_copies + spec_copies + den_copies + map_copies + part_copies + sum_copies
              + gathers):
        c.wait_send()


def exchange(ext, spec, den, response):
    pixels = ext.shape[1] - 2 * LB
    np_, nc = lax.axis_size("pix"), lax.axis_size("chan")
    lines = response.shape[0] // np_
    vmem = pl.BlockSpec(memory_space=pltpu.VMEM)
    sems = lambda n: pltpu.SemaphoreType.DMA((2, n))
    box = lambda *shape: pltpu.VMEM(shape, jnp.float32)
    return pl.pallas_call(
        functools.partial(exchange_kernel, np_, nc),
        in_specs=[vmem] * 4,
        out_specs=[vmem] * 3,
        out_shape=(
            jax.ShapeDtypeStruct((K, pixels), jnp.float32),
            jax.ShapeDtypeStruct((np_, 2 * K, lines), jnp.float32),
            jax.ShapeDtypeStruct(den.shape, jnp.float32),
        ),
        scratch_shapes=[
            box(K, pixels),
            box(2, K, LB),
            box(nc - 1, K, pixels // nc),
            box(np_, *spec.shape),
            box(nc, 2 * K, lines),
            box(nc, *den.shape),
            sems(2),
            sems(nc - 1),
            sems(nc - 1),
            sems(np_ - 1),
            sems(nc - 1),
            sems(nc - 1),
            sems(np_ - 1),
        ],
        compiler_params=pltpu.CompilerParams(
            collective_id=0, has_side_effects=True, vmem_limit_bytes=40 * 2**20
        ),
        name="exchange",
    )(ext, spec, den, response)


def shifts(axis):
    count = lax.axis_size(axis)
    up = [(i, i + 1) for i in range(count - 1)]
    return up, [(j, i) for i, j in up]


def body(counts, templates, spectra, response, psf_shape, widths):
    high = lax.Precision.HIGHEST
    pixels = templates.shape[1]
    channels = counts.shape[1]
    bands = channels // CB
    kernel = kernels(psf_shape, widths)
    kernel_here = lax.dynamic_slice_in_dim(kernel, lax.axis_index("chan") * bands, bands, 0)
    krev = jnp.pad(kernel_here[:, ::-1], ((0, 0), (0, 2 * LB - TAPS)))
    fold = jnp.dot(spectra, response, precision=high)
    own_band = (jnp.arange(bands)[:, None] == jnp.arange(channels)[None, :] // CB).astype(
        jnp.float32
    )
    fold_diag = (own_band[:, None, :] * fold[None]).reshape(bands * K, channels)
    up, down = shifts("pix")
    before = lax.ppermute(templates[:, pixels - HW :], "pix", up)
    after = lax.ppermute(templates[:, :HW], "pix", down)
    tp = jnp.concatenate(
        [before, templates, after, jnp.zeros((K, 2 * LB - 2 * HW), jnp.float32)], axis=1
    )
    ext, num, tot = sweep(tp, krev, fold_diag, counts, min(pixels, 2048))

    numerators = jnp.sum(num.reshape(bands, K, channels) * own_band[:, None, :], axis=0)
    totals = jnp.repeat(jnp.sum(tot, axis=1).reshape(bands, K).T, CB, axis=1)
    whole = pixels * lax.axis_size("pix")
    first = lax.axis_index("pix") * pixels
    spots = jnp.arange(LB, dtype=jnp.int32)
    local = jnp.where(spots < 2 * HW, spots, pixels - LB + spots)
    reach = first + local[None, :] + jnp.arange(TAPS, dtype=jnp.int32)[:, None] - HW
    inside = ((reach >= 0) & (reach < whole)).astype(jnp.float32)
    mass = jnp.dot(kernel_here, inside, precision=high)
    weight = jnp.sum(fold.reshape(K, bands, CB), axis=2)
    den = jnp.dot(weight, mass, precision=high)

    own, both, den = exchange(
        ext, jnp.concatenate([numerators, totals], axis=0), den, response
    )
    both = jnp.transpose(both, (1, 0, 2)).reshape(2 * K, response.shape[0])
    new_spectra = spectra * both[:K] / both[K:]
    den_map = jnp.concatenate(
        [
            den[:, :HW],
            jnp.broadcast_to(den[:, HW : HW + 1], (K, pixels - 2 * HW)),
            den[:, LB - HW :],
        ],
        axis=1,
    )
    new_templates = templates * own / den_map
    return (new_templates, new_spectra)


def solution(mesh):
    in_specs = (P("pix", "chan"), P(None, "pix"), P(), P(None, "chan"), P(), P())
    out_specs = (P(None, "pix"), P())
    return jax.shard_map(body, mesh=mesh, in_specs=in_specs, out_specs=out_specs, check_vma=False)
```

```python
import functools

import jax
import jax.numpy as jnp
from jax import lax
from jax.experimental import pallas as pl
from jax.experimental.pallas import tpu as pltpu
from jax.sharding import PartitionSpec as P

K = 16
CB = 32
HW = 32
TAPS = 65
LB = 128


def kernels(psf_shape, widths):
    offsets = jnp.arange(TAPS, dtype=jnp.int32) - HW
    in_band = jnp.abs(offsets)[None, :] <= widths[:, None]
    unscaled = jnp.where(in_band, psf_shape, jnp.float32(0.0))
    return unscaled / jnp.sum(unscaled, axis=1, keepdims=True)


def split(x):
    hi = x.astype(jnp.bfloat16)
    lo = (x - hi.astype(jnp.float32)).astype(jnp.bfloat16)
    return hi, lo


def dot(a, b, contract):
    return lax.dot_general(a, b, (contract, ((), ())), preferred_element_type=jnp.float32)


def dot3(a, b, contract):
    rows = a[0].shape[0]
    both = dot(jnp.concatenate([a[0], a[1]], axis=0), b[0], contract)
    return both[:rows] + both[rows:] + dot(a[0], b[1], contract)


def sweep_kernel(bands, tile, tp_ref, krev_ref, fold_ref, counts_ref, ext_ref, num_ref, tot_ref,
                 bhi, blo, fhl):
    step = pl.program_id(0)
    blocks = tile // LB
    rows = bands * K

    @pl.when(step == 0)
    def _():
        for b in range(bands):
            grid = jnp.broadcast_to(krev_ref[b : b + 1, :], (LB, 2 * LB))
            skew = pltpu.roll(grid, 0, 1, stride=1, stride_axis=0)
            hi, lo = split(skew)
            bhi[b * LB : (b + 1) * LB, :] = hi
            blo[b * LB : (b + 1) * LB, :] = lo
        fhi, flo = split(fold_ref[...])
        fhl[0:rows, :] = fhi
        fhl[rows : 2 * rows, :] = flo
        ext_ref[...] = jnp.zeros_like(ext_ref)
        num_ref[...] = jnp.zeros_like(num_ref)
        tot_ref[...] = jnp.zeros_like(tot_ref)

    at = pl.multiple_of(step * tile, tile)
    strip = tp_ref[:, pl.ds(at, tile + LB)]
    win = jnp.concatenate([strip[:, n * LB : (n + 2) * LB] for n in range(blocks)], axis=0)
    blur = dot3(split(win), (bhi[...], blo[...]), ((1,), (1,)))
    x = jnp.concatenate(
        [
            jnp.concatenate(
                [blur[n * K : (n + 1) * K, b * LB : (b + 1) * LB] for n in range(blocks)], axis=1
            )
            for b in range(bands)
        ],
        axis=0,
    )
    tot = x[:, 0:LB]
    for n in range(1, blocks):
        tot = tot + x[:, n * LB : (n + 1) * LB]
    tot_ref[...] += tot
    xs = split(x)
    fhi = fhl[0:rows, :]
    flo = fhl[rows : 2 * rows, :]
    xt = jnp.concatenate([xs[0], xs[1]], axis=0)
    predicted = dot(xt, jnp.concatenate([fhi, fhi], axis=0), ((0,), (0,))) + dot(
        xs[0], flo, ((0,), (0,))
    )
    ratios = split(counts_ref[...].astype(jnp.float32) / predicted)
    num_ref[...] += dot3(xs, ratios, ((1,), (0,)))
    back = dot3((fhi, flo), ratios, ((1,), (1,)))
    rearranged = jnp.concatenate(
        [
            jnp.concatenate(
                [back[b * K : (b + 1) * K, n * LB : (n + 1) * LB] for b in range(bands)], axis=1
            )
            for n in range(blocks)
        ],
        axis=0,
    )
    spread = dot3(split(rearranged), (bhi[...], blo[...]), ((1,), (0,)))
    pieces = []
    for n in range(blocks + 1):
        left = spread[n * K : (n + 1) * K, 0:LB] if n < blocks else None
        right = spread[(n - 1) * K : n * K, LB : 2 * LB] if n > 0 else None
        pieces.append(left if right is None else right if left is None else left + right)
    ext_ref[:, pl.ds(at, tile + LB)] += jnp.concatenate(pieces, axis=1)


def sweep(tp, krev, fold, counts, tile):
    pixels, channels = counts.shape
    bands = krev.shape[0]
    rows = bands * K
    full = lambda a: pl.BlockSpec(a.shape, lambda i: (0, 0))
    outs = (
        jax.ShapeDtypeStruct((K, pixels + 2 * LB), jnp.float32),
        jax.ShapeDtypeStruct((rows, channels), jnp.float32),
        jax.ShapeDtypeStruct((rows, LB), jnp.float32),
    )
    return pl.pallas_call(
        functools.partial(sweep_kernel, bands, tile),
        grid=(pixels // tile,),
        in_specs=[
            full(tp),
            full(krev),
            full(fold),
            pl.BlockSpec((tile, channels), lambda i: (i, 0)),
        ],
        out_specs=[full(o) for o in outs],
        out_shape=outs,
        scratch_shapes=[
            pltpu.VMEM((bands * LB, 2 * LB), jnp.bfloat16),
            pltpu.VMEM((bands * LB, 2 * LB), jnp.bfloat16),
            pltpu.VMEM((2 * rows, channels), jnp.bfloat16),
        ],
        compiler_params=pltpu.CompilerParams(vmem_limit_bytes=50 * 2**20),
        name="sweep",
    )(tp, krev, fold, counts)


def remote(src, dst, sems, slot, axis, to):
    return pltpu.make_async_remote_copy(
        src_ref=src,
        dst_ref=dst,
        send_sem=sems.at[0, slot],
        recv_sem=sems.at[1, slot],
        device_id={axis: to},
        device_id_type=pl.DeviceIdType.MESH,
    )


def exchange_kernel(np_, nc, ext_ref, spec_ref, den_ref, resp_ref, map_ref, sum_ref,
                    dsum_ref, own_ref, edge_slots, map_slots, spec_slots, part_slots,
                    den_slots, edge_sems, map_sems, gather_sems, spec_sems, part_sems,
                    den_sems, sum_sems):
    ip = lax.axis_index("pix")
    ic = lax.axis_index("chan")
    pixels = own_ref.shape[1]
    share = pixels // nc
    lines = resp_ref.shape[0] // np_
    barrier = pltpu.get_barrier_semaphore()
    for s in range(1, np_):
        pl.semaphore_signal(barrier, inc=1, device_id={"pix": lax.rem(ip + s, np_)},
                            device_id_type=pl.DeviceIdType.MESH)
    for s in range(1, nc):
        pl.semaphore_signal(barrier, inc=1, device_id={"chan": lax.rem(ic + s, nc)},
                            device_id_type=pl.DeviceIdType.MESH)
    pl.semaphore_wait(barrier, np_ + nc - 2)

    edge_copies = [
        remote(ext_ref.at[:, 0:LB], edge_slots.at[0], edge_sems, 0, "pix",
               lax.rem(ip + np_ - 1, np_)),
        remote(ext_ref.at[:, pixels : pixels + LB], edge_slots.at[1], edge_sems, 1, "pix",
               lax.rem(ip + 1, np_)),
    ]
    spec_copies = [
        remote(spec_ref, spec_slots.at[ip], spec_sems, s - 1, "pix", lax.rem(ip + s, np_))
        for s in range(1, np_)
    ]
    den_copies = [
        remote(den_ref, den_slots.at[ic], den_sems, s - 1, "chan", lax.rem(ic + s, nc))
        for s in range(1, nc)
    ]
    part_copies = [
        remote(part_slots.at[ic], part_slots.at[ic], part_sems, s - 1, "chan", lax.rem(ic + s, nc))
        for s in range(1, nc)
    ]
    sum_copies = [
        remote(sum_ref.at[ip], sum_ref.at[ip], sum_sems, s - 1, "pix", lax.rem(ip + s, np_))
        for s in range(1, np_)
    ]
    for c in edge_copies + spec_copies + den_copies:
        c.start()
    own_ref[...] = ext_ref[:, HW : pixels + HW]
    spec_slots[ip] = spec_ref[...]
    den_slots[ic] = den_ref[...]
    for c in edge_copies:
        c.wait_recv()
    has_left = jnp.where(ip > 0, 1.0, 0.0).astype(jnp.float32)
    has_right = jnp.where(ip < np_ - 1, 1.0, 0.0).astype(jnp.float32)
    own_ref[:, 0:HW] += edge_slots[1][:, HW : 2 * HW] * has_left
    own_ref[:, pixels - HW : pixels] += edge_slots[0][:, 0:HW] * has_right

    def piece(i):
        return pl.ds(pl.multiple_of(i * share, share), share)

    map_copies = []
    for s in range(1, nc):
        to = lax.rem(ic + s, nc)
        map_copies.append(
            remote(own_ref.at[:, piece(to)], map_slots.at[s - 1], map_sems, s - 1, "chan", to)
        )
    for c in map_copies:
        c.start()

    def spectral_terms():
        for c in spec_copies:
            c.wait_recv()
        spec = spec_slots[0]
        for i in range(1, np_):
            spec = spec + spec_slots[i]
        here = resp_ref[pl.ds(pl.multiple_of(ip * lines, lines), lines), :]
        part_slots[ic] = dot3(split(spec), split(here), ((1,), (1,)))
        for c in part_copies:
            c.start()

    def spectral_sums():
        for c in part_copies + den_copies:
            c.wait_recv()
        total = part_slots[0]
        den = den_slots[0]
        for i in range(1, nc):
            total = total + part_slots[i]
            den = den + den_slots[i]
        sum_ref[ip] = total
        dsum_ref[...] = den
        for c in sum_copies:
            c.start()

    spectral_terms()
    for c in map_copies:
        c.wait_recv()
    mine = own_ref[:, piece(ic)]
    for s in range(nc - 1):
        mine = mine + map_slots[s]
    map_ref[:, piece(ic)] = mine
    gathers = [
        remote(map_ref.at[:, piece(ic)], map_ref.at[:, piece(ic)], gather_sems, s - 1, "chan",
               lax.rem(ic + s, nc))
        for s in range(1, nc)
    ]
    for c in gathers:
        c.start()
    spectral_sums()
    for c in sum_copies + gathers:
        c.wait_recv()
    for c in (edge_copies + spec_copies + den_copies + map_copies + part_copies + sum_copies
              + gathers):
        c.wait_send()


def exchange(ext, spec, den, response):
    pixels = ext.shape[1] - 2 * LB
    np_, nc = lax.axis_size("pix"), lax.axis_size("chan")
    lines = response.shape[0] // np_
    vmem = pl.BlockSpec(memory_space=pltpu.VMEM)
    sems = lambda n: pltpu.SemaphoreType.DMA((2, n))
    box = lambda *shape: pltpu.VMEM(shape, jnp.float32)
    return pl.pallas_call(
        functools.partial(exchange_kernel, np_, nc),
        in_specs=[vmem] * 4,
        out_specs=[vmem] * 3,
        out_shape=(
            jax.ShapeDtypeStruct((K, pixels), jnp.float32),
            jax.ShapeDtypeStruct((np_, 2 * K, lines), jnp.float32),
            jax.ShapeDtypeStruct(den.shape, jnp.float32),
        ),
        scratch_shapes=[
            box(K, pixels),
            box(2, K, LB),
            box(nc - 1, K, pixels // nc),
            box(np_, *spec.shape),
            box(nc, 2 * K, lines),
            box(nc, *den.shape),
            sems(2),
            sems(nc - 1),
            sems(nc - 1),
            sems(np_ - 1),
            sems(nc - 1),
            sems(nc - 1),
            sems(np_ - 1),
        ],
        compiler_params=pltpu.CompilerParams(
            collective_id=0, has_side_effects=True, vmem_limit_bytes=40 * 2**20
        ),
        name="exchange",
    )(ext, spec, den, response)


def shifts(axis):
    count = lax.axis_size(axis)
    up = [(i, i + 1) for i in range(count - 1)]
    return up, [(j, i) for i, j in up]


def body(counts, templates, spectra, response, psf_shape, widths):
    high = lax.Precision.HIGHEST
    pixels = templates.shape[1]
    channels = counts.shape[1]
    bands = channels // CB
    kernel = kernels(psf_shape, widths)
    kernel_here = lax.dynamic_slice_in_dim(kernel, lax.axis_index("chan") * bands, bands, 0)
    krev = jnp.pad(kernel_here[:, ::-1], ((0, 0), (0, 2 * LB - TAPS)))
    fold = jnp.dot(spectra, response, precision=high)
    own_band = (jnp.arange(bands)[:, None] == jnp.arange(channels)[None, :] // CB).astype(
        jnp.float32
    )
    fold_diag = (own_band[:, None, :] * fold[None]).reshape(bands * K, channels)
    up, down = shifts("pix")
    before = lax.ppermute(templates[:, pixels - HW :], "pix", up)
    after = lax.ppermute(templates[:, :HW], "pix", down)
    tp = jnp.concatenate(
        [before, templates, after, jnp.zeros((K, 2 * LB - 2 * HW), jnp.float32)], axis=1
    )
    ext, num, tot = sweep(tp, krev, fold_diag, counts, min(pixels, 4096))

    numerators = jnp.sum(num.reshape(bands, K, channels) * own_band[:, None, :], axis=0)
    totals = jnp.repeat(jnp.sum(tot, axis=1).reshape(bands, K).T, CB, axis=1)
    whole = pixels * lax.axis_size("pix")
    first = lax.axis_index("pix") * pixels
    spots = jnp.arange(LB, dtype=jnp.int32)
    local = jnp.where(spots < 2 * HW, spots, pixels - LB + spots)
    reach = first + local[None, :] + jnp.arange(TAPS, dtype=jnp.int32)[:, None] - HW
    inside = ((reach >= 0) & (reach < whole)).astype(jnp.float32)
    mass = jnp.dot(kernel_here, inside, precision=high)
    weight = jnp.sum(fold.reshape(K, bands, CB), axis=2)
    den = jnp.dot(weight, mass, precision=high)

    own, both, den = exchange(
        ext, jnp.concatenate([numerators, totals], axis=0), den, response
    )
    both = jnp.transpose(both, (1, 0, 2)).reshape(2 * K, response.shape[0])
    new_spectra = spectra * both[:K] / both[K:]
    den_map = jnp.concatenate(
        [
            den[:, :HW],
            jnp.broadcast_to(den[:, HW : HW + 1], (K, pixels - 2 * HW)),
            den[:, LB - HW :],
        ],
        axis=1,
    )
    new_templates = templates * own / den_map
    return (new_templates, new_spectra)


def solution(mesh):
    in_specs = (P("pix", "chan"), P(None, "pix"), P(), P(None, "chan"), P(), P())
    out_specs = (P(None, "pix"), P())
    return jax.shard_map(body, mesh=mesh, in_specs=in_specs, out_specs=out_specs, check_vma=False)
```
